32 devices in a mesh: slab: 8 (over y, x, core), tomo: 4 (over z).
Axes of the slice: x: 2, y: 2, z: 4, core: 2. Of those that a mesh axis runs over, the one named last changes fastest.
Arguments:
- tomogram: bfloat16 [4, 128, 256, 256], P('tomo', 'slab'), may hold values from -6 to 6
- centers: int32 [4, 3, 256], P('tomo', None, 'slab'), may hold values from 0 to 240, as said below
- owner: int32 [4, 256], P('tomo', 'slab'), may hold values from -1 to 7, as said below
- rotation: int32 [4, 256], P('tomo', 'slab'), may hold values from 0 to 31
- ctf: float32 [4, 32, 1024], P('tomo'), may hold values from -1 to 1
- ref_spectra: float32 [32, 2, 32, 1024], replicated, may hold values from -6 to 6
Outputs:
- score: float32 [4, 128], P('tomo', 'slab')
- new_reference: float32 [32, 2, 32, 1024], replicated
The draws below stay inside these ranges and needn't reach their ends.
Inputs may be any that keep to these rules, and one draw needn't show every extreme that they name: The z center of a slot held by slab index s lies in [s * 16, (s + 1) * 16); x centers lie in [16, 240] and y centers in [16, 240]. Among the slots held by one slab index, each owner is named by 0 or exactly 4 slots; each owner is named by exactly 16 slots of its tomogram.
All inputs are finite; a program needn't handle non-finite values.
Results may differ from the reference program's by a relative error of at most 0.0003.
Values may be sent and summed in bfloat16 or wider, within the bound.
A program may use at most 320 MiB of HBM per device.

```python
import jax
import jax.numpy as jnp
from jax import lax

BOX = 32
NREF = 32
TX = 256
TY = 256
SZ = 16
NTOMO = 4
NZ = 128
CAP = 4
MOST = 32
PARTS_SIZE = 256
ALIGNED = 128
N_SLAB = 8


def owner_table(key):
    first_key, second_key = jax.random.split(key)
    source_order = jax.random.permutation(first_key, N_SLAB)
    placement = jnp.argsort(source_order).astype(jnp.int32)
    hot_count = N_SLAB // 4
    keep_count = N_SLAB // 2
    cold_span = N_SLAB - hot_count
    cold_keep = keep_count - hot_count
    targets = jnp.arange(N_SLAB, dtype=jnp.int32)
    cold_place = placement - hot_count
    active = (placement[:, None] < hot_count) | ((cold_place[:, None] - targets[None, :] * cold_keep) % cold_span < cold_keep)
    labels = jnp.where(active, targets[None, :], -1)
    labels = jnp.repeat(labels, CAP, axis=1)
    row_keys = jax.random.split(second_key, N_SLAB)
    shuffled = jax.vmap(jax.random.permutation)(row_keys, labels)
    return shuffled.reshape(PARTS_SIZE).astype(jnp.int32)


def draw_owner(key, part):
    key = jax.random.fold_in(key, 11)
    tomo_keys = jax.random.split(key, NTOMO)
    return jax.vmap(owner_table)(tomo_keys)


def draw_centers(key, part):
    key = jax.random.fold_in(key, 23)
    depth_key, row_key, col_key = jax.random.split(key, 3)
    slab_of = jnp.arange(PARTS_SIZE, dtype=jnp.int32) // MOST
    depth_at = slab_of[None, :] * SZ + jax.random.randint(depth_key, (NTOMO, PARTS_SIZE), 0, SZ)
    row_at = jax.random.randint(row_key, (NTOMO, PARTS_SIZE), BOX // 2, TX - BOX // 2 + 1)
    col_at = jax.random.randint(col_key, (NTOMO, PARTS_SIZE), BOX // 2, TY - BOX // 2 + 1)
    return jnp.stack((depth_at, row_at, col_at), axis=1).astype(jnp.int32)


def plant(result, key, low, largest):
    place = [jax.random.randint(jax.random.fold_in(key, axis), (), 0, length) for axis, length in enumerate(result.shape)]
    longest = result.shape.index(max(result.shape))
    beside = place[:longest] + [(place[longest] + 1) % result.shape[longest]] + place[longest + 1:]
    return result.at[tuple(place)].set(low).at[tuple(beside)].set(largest)


def block_levels(own_key, dims, pieces, least, high):
    def one(dim, parts):
        draws = jax.random.uniform(jax.random.fold_in(jax.random.fold_in(own_key, 6), dim), (parts,), jnp.float32, least / len(pieces), high / len(pieces))
        return jnp.repeat(jnp.exp(draws), dims[dim] // parts).reshape((-1,) + (1,) * (len(dims) - dim - 1))

    level = one(*pieces[0])
    for cut in pieces[1:]:
        level = level * one(*cut)
    return level


def noise(key, dims, deviation, reach, cuts=(), kind=jnp.bfloat16):
    level = block_levels(key, dims, cuts, -0.22, 0.18) if cuts else 1.0
    entries = jax.random.normal(key, dims, jnp.float32) * deviation * level
    return jnp.minimum(jnp.maximum(entries, -reach), reach).astype(kind)


def setup_inputs(seed: int = 0) -> dict:
    splits = jax.random.split(jax.random.key(seed), 7)
    return {
        "tomogram": noise(splits[0], (NTOMO, NZ, TX, TY), 1.0, 6.0, ((0, 4), (1, 8))),
        "centers": draw_centers(jax.random.fold_in(splits[6], 71), 0),
        "owner": draw_owner(jax.random.fold_in(splits[6], 71), 0),
        "rotation": plant(jax.random.randint(splits[3], (NTOMO, PARTS_SIZE), 0, NREF), jax.random.fold_in(splits[3], 1), 0, NREF - 1).astype(jnp.int32),
        "ctf": jnp.clip(jax.random.uniform(splits[4], (NTOMO, BOX, BOX * BOX), jnp.float32, -1.0, 1.0) * block_levels(splits[4], (NTOMO, BOX, BOX * BOX), ((0, 4),), -0.4, 0.0), -1.0, 1.0),
        "ref_spectra": noise(splits[5], (NREF, 2, BOX, BOX * BOX), 1.0, 6.0, (), jnp.float32),
    }


def reference(tomogram, centers, owner, rotation, ctf, ref_spectra):
    half_box = BOX // 2
    cell_count = BOX ** 3
    block_size = 64
    block_total = PARTS_SIZE // block_size
    ref_real_in = ref_spectra[:, 0].reshape(NREF, BOX, BOX, BOX)
    ref_imag_in = ref_spectra[:, 1].reshape(NREF, BOX, BOX, BOX)
    ref_hat = ref_real_in + 1j * ref_imag_in
    ref_power = lax.optimization_barrier(jnp.sum(ref_real_in * ref_real_in + ref_imag_in * ref_imag_in, axis=(1, 2, 3)))

    def per_tomogram(carry_in, inputs):
        num_real, num_imag, denominator = carry_in
        volume_in, centers_t, owner_t, rotation_t, ctf_t = inputs
        volume = jnp.pad(volume_in.astype(jnp.float32), ((half_box, half_box), (0, 0), (0, 0)))
        weights_grid = ctf_t.reshape(BOX, BOX, BOX)

        def cut_box(depth_at, row_at, col_at):
            return lax.dynamic_slice(volume, (depth_at, row_at - half_box, col_at - half_box), (BOX, BOX, BOX))

        def per_block(block_carry, block_inputs):
            sum_real, sum_imag, counts = block_carry
            depth_at, row_at, col_at, block_rot, block_live = block_inputs
            boxes = jax.vmap(cut_box)(depth_at, row_at, col_at)
            spectra = weights_grid[None] * jnp.fft.fftn(boxes, axes=(1, 2, 3), norm='ortho')
            chosen = ref_hat[block_rot]
            cross = jnp.real(jnp.fft.ifftn(spectra * jnp.conj(chosen), axes=(1, 2, 3), norm='ortho'))
            own_power = lax.optimization_barrier(jnp.sum(jnp.real(spectra) ** 2 + jnp.imag(spectra) ** 2, axis=(1, 2, 3)))
            scores = cell_count * lax.optimization_barrier(jnp.max(cross, axis=(1, 2, 3))) / jnp.sqrt(own_power * ref_power[block_rot] + 1e-06)
            members = ((block_rot[:, None] == jnp.arange(NREF, dtype=jnp.int32)[None, :]) & block_live[:, None]).astype(jnp.float32)
            sum_real = sum_real + jnp.einsum('sr,sabc->rabc', members, jnp.real(spectra))
            sum_imag = sum_imag + jnp.einsum('sr,sabc->rabc', members, jnp.imag(spectra))
            counts = counts + lax.optimization_barrier(jnp.sum(members, axis=0))
            return ((sum_real, sum_imag, counts), scores)
        block_inputs = (centers_t[0].reshape(block_total, block_size), centers_t[1].reshape(block_total, block_size), centers_t[2].reshape(block_total, block_size), rotation_t.reshape(block_total, block_size), (owner_t >= 0).reshape(block_total, block_size))
        start_counts = jnp.zeros((NREF,), jnp.float32)
        (num_real, num_imag, counts), scores = lax.scan(per_block, (num_real, num_imag, start_counts), block_inputs)
        denominator = denominator + counts[:, None] * (ctf_t * ctf_t).reshape(1, cell_count)
        slot_index = jnp.arange(PARTS_SIZE, dtype=jnp.int32)
        sort_key = jnp.where(owner_t >= 0, owner_t * PARTS_SIZE + slot_index, N_SLAB * PARTS_SIZE + slot_index)
        live_order = jnp.argsort(sort_key, stable=True)[:ALIGNED]
        aligned = scores.reshape(PARTS_SIZE)[live_order]
        return ((num_real, num_imag, denominator), aligned)
    start = (jnp.zeros((NREF, BOX, BOX, BOX), jnp.float32), jnp.zeros((NREF, BOX, BOX, BOX), jnp.float32), jnp.zeros((NREF, cell_count), jnp.float32))
    (num_real, num_imag, denominator), score = lax.scan(per_tomogram, start, (tomogram, centers, owner, rotation, ctf))
    stacked = jnp.stack((num_real, num_imag), axis=1).reshape(NREF, 2, BOX, BOX * BOX)
    new_reference = stacked / (denominator.reshape(NREF, 1, BOX, BOX * BOX) + 1.0)
    return (score, new_reference)
```

```python
import functools
import math

import jax
import jax.numpy as jnp
import ml_dtypes
import numpy as np
from jax import lax
from jax.experimental import pallas as pl
from jax.experimental.pallas import tpu as pltpu
from jax.sharding import PartitionSpec as P

GROUP = 8
LIMIT = 56 * 1024 * 1024


def split_table(table):
    high = table.astype(ml_dtypes.bfloat16)
    low = (table - high.astype(np.float64)).astype(ml_dtypes.bfloat16)
    return high, low


def plane_tables(length):
    n = np.arange(length)
    angles = 2.0 * math.pi / length * (np.outer(n, n) % length)
    one = (np.cos(angles) - 1j * np.sin(angles)) / math.sqrt(length)
    both = np.kron(one, one)
    table = np.concatenate((both.real, both.imag), axis=1)
    return np.stack(split_table(table))


def depth_tables(length):
    n = np.arange(length)
    angles = 2.0 * math.pi / length * (np.outer(n, n) % length)
    c = np.cos(angles) / math.sqrt(length)
    s = np.sin(angles) / math.sqrt(length)
    result = []
    for sign in (1.0, -1.0):
        high, low = split_table(np.block([[c, sign * s], [-sign * s, c]]))
        result.append(np.concatenate((high, high, low), axis=1))
    return np.stack(result)


def split(x):
    high = x.astype(jnp.bfloat16)
    return high, (x - high.astype(jnp.float32)).astype(jnp.bfloat16)


def dot(a, b):
    return jnp.dot(a, b, preferred_element_type=jnp.float32)


def depth_pass(table, x):
    high, low = split(x)
    return dot(table, jnp.concatenate((high, low, high), axis=0))


def cut_kernel(info, below, here, above, boxes, sums, volume, window, sems):
    depth, rows, cols = here.shape
    slots, box_len, _ = boxes.shape
    span = box_len + 16
    half = below.shape[0]
    copies = [
        pltpu.make_async_copy(below, volume.at[pl.ds(0, half)], sems.at[0]),
        pltpu.make_async_copy(here, volume.at[pl.ds(half, depth)], sems.at[1]),
        pltpu.make_async_copy(above, volume.at[pl.ds(half + depth, half)], sems.at[2]),
    ]
    for copy in copies:
        copy.start()
    sums[...] = jnp.zeros_like(sums)
    for copy in copies:
        copy.wait()
    lane = lax.broadcasted_iota(jnp.int32, (cols, 128), 1)
    source = lax.broadcasted_iota(jnp.int32, (cols, 128), 0)
    quarter = lax.broadcasted_iota(jnp.int32, (box_len, 128), 1) // box_len

    @pl.loop(0, slots)
    def _(i):
        z0 = info[0, i]
        x0 = info[1, i]
        y0 = info[2, i]
        rot = info[3, i]
        live = info[4, i]
        start = pl.multiple_of(jnp.minimum(x0 // 16 * 16, rows - span), 16)
        pick = (source == y0 + lane % box_len).astype(jnp.float32).astype(jnp.bfloat16)
        cells = volume[pl.ds(z0, box_len), pl.ds(start, span), :]
        window[...] = dot(cells.reshape(box_len * span, cols), pick)
        shift = x0 - start
        for q in range(box_len * box_len // 128):
            part = jnp.zeros((box_len, 128), jnp.float32)
            for e in range(128 // box_len):
                got = window[pl.ds(shift + q * (128 // box_len) + e, box_len, stride=span), :]
                part = jnp.where(quarter == e, got, part)
            lanes = pl.ds(q * 128, 128)
            boxes[i, :, lanes] = part.astype(jnp.bfloat16)

            @pl.when(live > 0)
            def _():
                sums[rot, :, lanes] += part


def score_kernel(rot, boxes, refs, ctf, plane, depth, out, spec, back_high, back_low):
    slots, box_len, cells = boxes.shape
    rows = GROUP * box_len

    @pl.loop(0, slots // GROUP)
    def _(g):
        b = boxes[pl.ds(g * GROUP, GROUP)].reshape(rows, cells)
        spec[...] = (dot(b, plane[0]) + dot(b, plane[1])).reshape(GROUP, box_len, 2 * cells)

        powers = []
        for j in range(GROUP):
            slot = g * GROUP + j
            ref_at = rot[slot]
            x = spec[j]
            x = jnp.concatenate((x[:, :cells], x[:, cells:]), axis=0)
            x = depth_pass(depth[0], x)
            weights = ctf[...]
            sr = x[:box_len] * weights
            si = x[box_len:] * weights
            rr = refs[ref_at, 0]
            ri = refs[ref_at, 1]
            own = jnp.sum(sr * sr + si * si, axis=(0, 1), keepdims=True)
            ref = jnp.sum(rr * rr + ri * ri, axis=(0, 1), keepdims=True)
            powers.append(own * ref)
            prod = jnp.concatenate((sr * rr + si * ri, si * rr - sr * ri), axis=0)
            high, low = split(depth_pass(depth[1], prod))
            at = pl.ds(j * box_len, box_len)
            back_high[at, :cells] = high[:box_len]
            back_high[at, cells:] = high[box_len:]
            back_low[at, :cells] = low[:box_len]
            back_low[at, cells:] = low[box_len:]

        cross = jnp.zeros((rows, cells), jnp.float32)
        for c in range(2):
            lanes = pl.ds(c * cells, cells)
            high = back_high[:, lanes]
            cross += dot(high, plane[0, :, lanes]) + dot(high, plane[1, :, lanes])
            cross += dot(back_low[:, lanes], plane[0, :, lanes])
        for j in range(GROUP):
            part = cross[j * box_len : (j + 1) * box_len]
            peak = jnp.max(part, axis=(0, 1), keepdims=True)
            score = (cells * box_len) * peak / jnp.sqrt(powers[j] + 1e-06)
            out[pl.ds(g * GROUP + j, 1), :] = jnp.broadcast_to(score, (1, 128))


def class_kernel(sums, ctf, plane, depth, out):
    count, box_len, cells = sums.shape
    high, low = split(sums[...].reshape(count * box_len, cells))
    x = dot(high, plane[0]) + dot(high, plane[1]) + dot(low, plane[0])
    for r in range(count):
        part = x[r * box_len : (r + 1) * box_len]
        part = jnp.concatenate((part[:, :cells], part[:, cells:]), axis=0)
        part = depth_pass(depth[0], part)
        at = pl.ds(r * box_len, box_len)
        out[0, at, :] = part[:box_len] * ctf[...]
        out[1, at, :] = part[box_len:] * ctf[...]


VMEM = pl.BlockSpec(memory_space=pltpu.VMEM)
SMEM = pl.BlockSpec(memory_space=pltpu.SMEM)
ANY = pl.BlockSpec(memory_space=pl.ANY)


def local(tomogram, centers, owner, rotation, ctf, ref_spectra, plane, depth):
    slab_count = lax.axis_size("slab")
    tomo_count = lax.axis_size("tomo")
    me = lax.axis_index("slab")
    ref_count, _, box_len, cells = ref_spectra.shape
    half = box_len // 2
    here = tomogram[0]
    slab_depth, rows, cols = here.shape
    slots = owner.shape[1]
    aligned = 16

    n = slab_count
    below = lax.ppermute(here[slab_depth - half :], "slab", [(i, i + 1) for i in range(n - 1)])
    above = lax.ppermute(here[:half], "slab", [(i + 1, i) for i in range(n - 1)])

    labels = jnp.stack((owner[0], rotation[0]))
    all_labels = lax.all_gather(labels, ("tomo", "slab"))
    all_labels = all_labels.reshape(tomo_count, slab_count, 2, slots)
    all_owner = all_labels[:, :, 0].reshape(tomo_count, slab_count * slots)
    all_rotation = all_labels[:, :, 1].reshape(tomo_count, slab_count * slots)
    all_ctf = lax.all_gather(ctf[0], "tomo")

    info = jnp.stack(
        (
            centers[0, 0] - me * slab_depth,
            centers[0, 1] - half,
            centers[0, 2] - half,
            rotation[0],
            (owner[0] >= 0).astype(jnp.int32),
        )
    )
    boxes, sums = pl.pallas_call(
        cut_kernel,
        out_shape=(
            jax.ShapeDtypeStruct((slots, box_len, cells), jnp.bfloat16),
            jax.ShapeDtypeStruct((ref_count, box_len, cells), jnp.float32),
        ),
        in_specs=[SMEM, ANY, ANY, ANY],
        out_specs=(VMEM, VMEM),
        scratch_shapes=[
            pltpu.VMEM((2 * half + slab_depth, rows, cols), jnp.bfloat16),
            pltpu.VMEM((box_len * (box_len + 16), 128), jnp.float32),
            pltpu.SemaphoreType.DMA((3,)),
        ],
        compiler_params=pltpu.CompilerParams(vmem_limit_bytes=LIMIT),
    )(info, below, here, above)

    mine = lax.psum_scatter(sums, "slab", scatter_dimension=0, tiled=True)

    scores = pl.pallas_call(
        score_kernel,
        out_shape=jax.ShapeDtypeStruct((slots, 128), jnp.float32),
        in_specs=[SMEM, VMEM, VMEM, VMEM, VMEM, VMEM],
        out_specs=VMEM,
        scratch_shapes=[
            pltpu.VMEM((GROUP, box_len, 2 * cells), jnp.float32),
            pltpu.VMEM((GROUP * box_len, 2 * cells), jnp.bfloat16),
            pltpu.VMEM((GROUP * box_len, 2 * cells), jnp.bfloat16),
        ],
        compiler_params=pltpu.CompilerParams(vmem_limit_bytes=LIMIT),
        cost_estimate=pl.CostEstimate(
            flops=2 * slots * box_len * cells * 2 * cells * 6, bytes_accessed=20 << 20, transcendentals=0
        ),
    )(rotation[0], boxes, ref_spectra, ctf[0], plane, depth)[:, 0]

    count = ref_count // slab_count
    spectra = pl.pallas_call(
        class_kernel,
        out_shape=jax.ShapeDtypeStruct((2, count * box_len, cells), jnp.float32),
        in_specs=[VMEM] * 4,
        out_specs=VMEM,
        compiler_params=pltpu.CompilerParams(vmem_limit_bytes=LIMIT),
        cost_estimate=pl.CostEstimate(
            flops=2 * count * box_len * cells * 2 * cells * 4, bytes_accessed=10 << 20, transcendentals=0
        ),
    )(mine, ctf[0], plane, depth)
    numer = lax.psum_scatter(spectra, "tomo", scatter_dimension=1, tiled=True)

    per = count * box_len // tomo_count
    first = lax.axis_index("tomo") * per
    r_at = me * count + first // box_len
    hits = (all_rotation == r_at) & (all_owner >= 0)
    times = jnp.sum(hits.astype(jnp.float32), axis=1)
    part_ctf = lax.dynamic_slice_in_dim(all_ctf, first % box_len, per, axis=1)
    weight = jnp.sum(times[:, None, None] * part_ctf * part_ctf, axis=0)
    result = numer / (weight + 1.0)

    largest = jnp.max(jnp.abs(result), axis=2, keepdims=True)
    scale = jnp.where(largest > 0, largest, 1.0) * (1.0 / 32767.0)
    coded = jnp.round(result / scale).astype(jnp.int16)
    coded = lax.all_gather(coded, ("slab", "tomo"))
    scale = lax.all_gather(scale[:, :, 0], ("slab", "tomo"))
    decoded = coded.astype(jnp.float32) * scale[:, :, :, None]
    decoded = decoded.reshape(ref_count, box_len // per, 2, per, cells)
    new_reference = jnp.swapaxes(decoded, 1, 2).reshape(ref_count, 2, box_len, cells)

    all_scores = lax.all_gather(scores, "slab").reshape(slab_count * slots)
    own = lax.dynamic_index_in_dim(all_owner, lax.axis_index("tomo"), 0, keepdims=False) == me
    rank = jnp.cumsum(own.astype(jnp.int32)) - 1
    chosen = own[None, :] & (rank[None, :] == jnp.arange(aligned, dtype=jnp.int32)[:, None])
    score = jnp.sum(jnp.where(chosen, all_scores[None, :], 0.0), axis=1)
    return score.reshape(1, aligned), new_reference


def solution(mesh):
    inner = jax.shard_map(
        local,
        mesh=mesh,
        in_specs=(
            P("tomo", "slab", None, None),
            P("tomo", None, "slab"),
            P("tomo", "slab"),
            P("tomo", "slab"),
            P("tomo", None, None),
            P(),
            P(),
            P(),
        ),
        out_specs=(P("tomo", "slab"), P()),
        check_vma=False,
    )

    def program(tomogram, centers, owner, rotation, ctf, ref_spectra):
        box_len = ref_spectra.shape[2]
        plane = jnp.asarray(plane_tables(box_len))
        depth = jnp.asarray(depth_tables(box_len))
        return inner(tomogram, centers, owner, rotation, ctf, ref_spectra, plane, depth)

    return program
```

```python
import functools
import math

import jax
import jax.numpy as jnp
import ml_dtypes
import numpy as np
from jax import lax
from jax.experimental import pallas as pl
from jax.experimental.pallas import tpu as pltpu
from jax.sharding import PartitionSpec as P

GROUP = 8
LIMIT = 56 * 1024 * 1024


def split_table(table):
    high = table.astype(ml_dtypes.bfloat16)
    low = (table - high.astype(np.float64)).astype(ml_dtypes.bfloat16)
    return high, low


def plane_tables(length):
    n = np.arange(length)
    angles = 2.0 * math.pi / length * (np.outer(n, n) % length)
    one = (np.cos(angles) - 1j * np.sin(angles)) / math.sqrt(length)
    both = np.kron(one, one)
    table = np.concatenate((both.real, both.imag), axis=1)
    return np.stack(split_table(table))


def depth_tables(length):
    n = np.arange(length)
    angles = 2.0 * math.pi / length * (np.outer(n, n) % length)
    c = np.cos(angles) / math.sqrt(length)
    s = np.sin(angles) / math.sqrt(length)
    result = []
    for sign in (1.0, -1.0):
        high, low = split_table(np.block([[c, sign * s], [-sign * s, c]]))
        result.append(np.concatenate((high, high, low), axis=1))
    return np.stack(result)


def split(x):
    high = x.astype(jnp.bfloat16)
    return high, (x - high.astype(jnp.float32)).astype(jnp.bfloat16)


def dot(a, b):
    return jnp.dot(a, b, preferred_element_type=jnp.float32)


def depth_pass(table, x):
    high, low = split(x)
    return dot(table, jnp.concatenate((high, low, high), axis=0))


def cut_kernel(info, below, here, above, boxes, sums, volume, window):
    depth, rows, cols = here.shape
    slots, box_len, _ = boxes.shape
    span = box_len + 16
    half = below.shape[0]
    sums[...] = jnp.zeros_like(sums)
    volume[:half] = below[...]
    volume[half : half + depth] = here[...]
    volume[half + depth :] = above[...]
    lane = lax.broadcasted_iota(jnp.int32, (cols, 128), 1)
    source = lax.broadcasted_iota(jnp.int32, (cols, 128), 0)
    quarter = lax.broadcasted_iota(jnp.int32, (box_len, 128), 1) // box_len

    @pl.loop(0, slots)
    def _(i):
        z0 = info[0, i]
        x0 = info[1, i]
        y0 = info[2, i]
        rot = info[3, i]
        live = info[4, i]
        start = pl.multiple_of(jnp.minimum(x0 // 16 * 16, rows - span), 16)
        pick = (source == y0 + lane % box_len).astype(jnp.float32).astype(jnp.bfloat16)
        cells = volume[pl.ds(z0, box_len), pl.ds(start, span), :]
        window[...] = dot(cells.reshape(box_len * span, cols), pick)
        shift = x0 - start
        for q in range(box_len * box_len // 128):
            part = jnp.zeros((box_len, 128), jnp.float32)
            for e in range(128 // box_len):
                got = window[pl.ds(shift + q * (128 // box_len) + e, box_len, stride=span), :]
                part = jnp.where(quarter == e, got, part)
            lanes = pl.ds(q * 128, 128)
            boxes[i, :, lanes] = part.astype(jnp.bfloat16)

            @pl.when(live > 0)
            def _():
                sums[rot, :box_len, lanes] += part

        @pl.when(live > 0)
        def _():
            sums[rot, box_len:, :] += 1.0


def score_kernel(rot, boxes, refs, ctf, plane, depth, out, spec, back_high, back_low):
    slots, box_len, cells = boxes.shape
    rows = GROUP * box_len

    @pl.loop(0, slots // GROUP)
    def _(g):
        b = boxes[pl.ds(g * GROUP, GROUP)].reshape(rows, cells)
        spec[...] = (dot(b, plane[0]) + dot(b, plane[1])).reshape(GROUP, box_len, 2 * cells)

        powers = []
        for j in range(GROUP):
            slot = g * GROUP + j
            ref_at = rot[slot]
            x = spec[j]
            x = jnp.concatenate((x[:, :cells], x[:, cells:]), axis=0)
            x = depth_pass(depth[0], x)
            weights = ctf[...]
            sr = x[:box_len] * weights
            si = x[box_len:] * weights
            rr = refs[ref_at, 0]
            ri = refs[ref_at, 1]
            own = jnp.sum(sr * sr + si * si, axis=(0, 1), keepdims=True)
            ref = jnp.sum(rr * rr + ri * ri, axis=(0, 1), keepdims=True)
            powers.append(own * ref)
            prod = jnp.concatenate((sr * rr + si * ri, si * rr - sr * ri), axis=0)
            high, low = split(depth_pass(depth[1], prod))
            at = pl.ds(j * box_len, box_len)
            back_high[at, :cells] = high[:box_len]
            back_high[at, cells:] = high[box_len:]
            back_low[at, :cells] = low[:box_len]
            back_low[at, cells:] = low[box_len:]

        cross = jnp.zeros((rows, cells), jnp.float32)
        for c in range(2):
            lanes = pl.ds(c * cells, cells)
            high = back_high[:, lanes]
            cross += dot(high, plane[0, :, lanes]) + dot(high, plane[1, :, lanes])
            cross += dot(back_low[:, lanes], plane[0, :, lanes])
        for j in range(GROUP):
            part = cross[j * box_len : (j + 1) * box_len]
            peak = jnp.max(part, axis=(0, 1), keepdims=True)
            score = (cells * box_len) * peak / jnp.sqrt(powers[j] + 1e-06)
            out[pl.ds(g * GROUP + j, 1), :] = jnp.broadcast_to(score, (1, 128))


def class_kernel(sums, ctf, plane, depth, out):
    count = sums.shape[0]
    box_len, cells = ctf.shape
    high, low = split(sums[:, :box_len, :].reshape(count * box_len, cells))
    x = dot(high, plane[0]) + dot(high, plane[1]) + dot(low, plane[0])
    for r in range(count):
        part = x[r * box_len : (r + 1) * box_len]
        part = jnp.concatenate((part[:, :cells], part[:, cells:]), axis=0)
        part = depth_pass(depth[0], part)
        at = pl.ds(r * box_len, box_len)
        out[0, at, :] = part[:box_len] * ctf[...]
        out[1, at, :] = part[box_len:] * ctf[...]
        out[2, at, :] = sums[r, box_len : box_len + 1, :] * ctf[...] * ctf[...]


def gather_kernel(slabs, tomos, chunk, labels, out, tags, send, arrive, tag_send, tag_arrive, local_sems):
    s = lax.axis_index("slab")
    t = lax.axis_index("tomo")
    pairs = slabs // 2
    parity = lax.rem(s, 2)
    pair = s // 2
    sibling = s + 1 - 2 * parity
    peers = [lax.rem(pair + d, pairs) * 2 + parity for d in range(1, pairs)]
    depths = [lax.rem(t + d, tomos) for d in range(1, tomos)]
    mates = [lax.rem(s + d, slabs) for d in range(1, slabs)]

    barrier = pltpu.get_barrier_semaphore()
    partners = [(s, d) for d in depths] + [(m, t) for m in mates]
    for place in partners:
        pl.semaphore_signal(barrier, inc=1, device_id=place, device_id_type=pl.DeviceIdType.MESH)
    pl.semaphore_wait(barrier, len(partners))

    started = []

    def push(source, at_s, at_t, place):
        copy = pltpu.make_async_remote_copy(
            src_ref=source,
            dst_ref=out.at[at_s, at_t],
            send_sem=send.at[len(started)],
            recv_sem=arrive.at[at_s, at_t],
            device_id=place,
            device_id_type=pl.DeviceIdType.MESH,
        )
        copy.start()
        started.append(copy)

    def landed(at_s, at_t):
        pltpu.make_async_remote_copy(
            src_ref=out.at[at_s, at_t],
            dst_ref=out.at[at_s, at_t],
            send_sem=send.at[0],
            recv_sem=arrive.at[at_s, at_t],
            device_id=(sibling, t),
            device_id_type=pl.DeviceIdType.MESH,
        ).wait_recv()

    own = pltpu.make_async_copy(chunk, out.at[s, t], local_sems.at[0])
    own.start()
    own_tag = pltpu.make_async_copy(labels, tags.at[s], local_sems.at[1])
    own_tag.start()
    for d in depths:
        push(chunk, s, t, (s, d))
    for p in peers:
        push(chunk, s, t, (p, t))
    push(chunk, s, t, (sibling, t))
    tag_copies = []
    for i, m in enumerate(mates):
        copy = pltpu.make_async_remote_copy(
            src_ref=labels,
            dst_ref=tags.at[s],
            send_sem=tag_send.at[i],
            recv_sem=tag_arrive.at[s],
            device_id=(m, t),
            device_id_type=pl.DeviceIdType.MESH,
        )
        copy.start()
        tag_copies.append(copy)
    for d in depths:
        landed(s, d)
        for p in peers:
            push(out.at[s, d], s, d, (p, t))
        push(out.at[s, d], s, d, (sibling, t))
    for d in [t] + depths:
        for p in peers:
            landed(p, d)
            push(out.at[p, d], p, d, (sibling, t))
    for d in [t] + depths:
        for p in [pair * 2 + 1 - parity] + [q + 1 - 2 * parity for q in peers]:
            landed(p, d)
    for m in mates:
        pltpu.make_async_remote_copy(
            src_ref=labels,
            dst_ref=tags.at[m],
            send_sem=tag_send.at[0],
            recv_sem=tag_arrive.at[m],
            device_id=(m, t),
            device_id_type=pl.DeviceIdType.MESH,
        ).wait_recv()
    own.wait()
    own_tag.wait()
    for copy in started + tag_copies:
        copy.wait_send()


VMEM = pl.BlockSpec(memory_space=pltpu.VMEM)
SMEM = pl.BlockSpec(memory_space=pltpu.SMEM)
ANY = pl.BlockSpec(memory_space=pl.ANY)


def local(tomogram, centers, owner, rotation, ctf, ref_spectra, plane, depth):
    slab_count = lax.axis_size("slab")
    tomo_count = lax.axis_size("tomo")
    me = lax.axis_index("slab")
    ref_count, _, box_len, cells = ref_spectra.shape
    half = box_len // 2
    here = tomogram[0]
    slab_depth, rows, cols = here.shape
    slots = owner.shape[1]
    aligned = 16

    n = slab_count
    below = lax.ppermute(here[slab_depth - half :], "slab", [(i, i + 1) for i in range(n - 1)])
    above = lax.ppermute(here[:half], "slab", [(i + 1, i) for i in range(n - 1)])

    info = jnp.stack(
        (
            centers[0, 0] - me * slab_depth,
            centers[0, 1] - half,
            centers[0, 2] - half,
            rotation[0],
            (owner[0] >= 0).astype(jnp.int32),
        )
    )
    boxes, sums = pl.pallas_call(
        cut_kernel,
        out_shape=(
            jax.ShapeDtypeStruct((slots, box_len, cells), jnp.bfloat16),
            jax.ShapeDtypeStruct((ref_count, box_len + 8, cells), jnp.float32),
        ),
        in_specs=[SMEM, VMEM, VMEM, VMEM],
        out_specs=(VMEM, VMEM),
        scratch_shapes=[
            pltpu.VMEM((2 * half + slab_depth, rows, cols), jnp.bfloat16),
            pltpu.VMEM((box_len * (box_len + 16), 128), jnp.float32),
        ],
        compiler_params=pltpu.CompilerParams(vmem_limit_bytes=LIMIT),
    )(info, below, here, above)

    mine = lax.psum_scatter(sums, "slab", scatter_dimension=0, tiled=True)

    score_call = lambda part: pl.pallas_call(
        score_kernel,
        out_shape=jax.ShapeDtypeStruct((part, 128), jnp.float32),
        in_specs=[SMEM, VMEM, VMEM, VMEM, VMEM, VMEM],
        out_specs=VMEM,
        scratch_shapes=[
            pltpu.VMEM((GROUP, box_len, 2 * cells), jnp.float32),
            pltpu.VMEM((GROUP * box_len, 2 * cells), jnp.bfloat16),
            pltpu.VMEM((GROUP * box_len, 2 * cells), jnp.bfloat16),
        ],
        compiler_params=pltpu.CompilerParams(vmem_limit_bytes=LIMIT),
        cost_estimate=pl.CostEstimate(
            flops=2 * part * box_len * cells * 2 * cells * 8, bytes_accessed=20 << 20, transcendentals=0
        ),
    )
    def score_part(i, length):
        return score_call(length)(
            rotation[0, i : i + length], boxes[i : i + length], ref_spectra, ctf[0], plane, depth
        )[:, 0]

    part = slots * 3 // 4
    early = score_part(0, part)
    mine, early = lax.optimization_barrier((mine, early))

    count = ref_count // slab_count
    spectra = pl.pallas_call(
        class_kernel,
        out_shape=jax.ShapeDtypeStruct((3, count * box_len, cells), jnp.float32),
        in_specs=[VMEM] * 4,
        out_specs=VMEM,
        compiler_params=pltpu.CompilerParams(vmem_limit_bytes=LIMIT),
        cost_estimate=pl.CostEstimate(
            flops=2 * count * box_len * cells * 2 * cells * 4, bytes_accessed=10 << 20, transcendentals=0
        ),
    )(mine, ctf[0], plane, depth)
    numer = lax.psum_scatter(spectra, "tomo", scatter_dimension=1, tiled=True)
    scores = jnp.concatenate((early, score_part(part, slots - part)))

    per = count * box_len // tomo_count
    result = numer[:2] / (numer[2:] + 1.0)

    largest = jnp.max(jnp.abs(result), axis=2, keepdims=True)
    power = jnp.floor(jnp.log2(jnp.maximum(largest, 2.0**-90))) - 13.0
    digits = jnp.ceil(largest / jnp.exp2(power))

    def row_scale(digits, power):
        return jnp.maximum(digits, 1.0) * jnp.exp2(power) * (1.0 / 32767.0)

    coded = jnp.clip(jnp.round(result / row_scale(digits, power)), -32767.0, 32767.0)
    lane = lax.broadcasted_iota(jnp.int32, (2, per, 128), 2)
    coded = jnp.concatenate((coded, jnp.where(lane == 0, digits, power)), axis=2)
    coded = coded.astype(jnp.int16).reshape(2 * per, cells + 128)
    labels = jnp.zeros((8, 128), jnp.float32).at[0, :slots].set(scores)
    labels = labels.at[1, :slots].set(owner[0].astype(jnp.float32))
    pairs = slab_count // 2
    sends = tomo_count - 1 + pairs + (tomo_count - 1) * pairs + tomo_count * (pairs - 1)
    gathered, tags = pl.pallas_call(
        functools.partial(gather_kernel, slab_count, tomo_count),
        out_shape=(
            jax.ShapeDtypeStruct((slab_count, tomo_count, 2 * per, cells + 128), jnp.int16),
            jax.ShapeDtypeStruct((slab_count, 8, 128), jnp.float32),
        ),
        in_specs=[ANY, ANY],
        out_specs=(ANY, ANY),
        scratch_shapes=[
            pltpu.SemaphoreType.DMA((sends,)),
            pltpu.SemaphoreType.DMA((slab_count, tomo_count)),
            pltpu.SemaphoreType.DMA((slab_count,)),
            pltpu.SemaphoreType.DMA((slab_count,)),
            pltpu.SemaphoreType.DMA((2,)),
        ],
        compiler_params=pltpu.CompilerParams(
            collective_id=0, has_side_effects=True, vmem_limit_bytes=LIMIT
        ),
    )(coded, labels)
    gathered = gathered.reshape(ref_count, box_len // per, 2, per, cells + 128)
    head = gathered[..., cells : cells + 2].astype(jnp.float32)
    scale = row_scale(head[..., :1], head[..., 1:])
    decoded = gathered[..., :cells].astype(jnp.float32) * scale
    new_reference = jnp.swapaxes(decoded, 1, 2).reshape(ref_count, 2, box_len, cells)

    all_scores = tags[:, 0, :slots].reshape(slab_count * slots)
    own = tags[:, 1, :slots].reshape(slab_count * slots).astype(jnp.int32) == me
    rank = jnp.cumsum(own.astype(jnp.int32)) - 1
    chosen = own[None, :] & (rank[None, :] == jnp.arange(aligned, dtype=jnp.int32)[:, None])
    score = jnp.sum(jnp.where(chosen, all_scores[None, :], 0.0), axis=1)
    return score.reshape(1, aligned), new_reference


def solution(mesh):
    inner = jax.shard_map(
        local,
        mesh=mesh,
        in_specs=(
            P("tomo", "slab", None, None),
            P("tomo", None, "slab"),
            P("tomo", "slab"),
            P("tomo", "slab"),
            P("tomo", None, None),
            P(),
            P(),
            P(),
        ),
        out_specs=(P("tomo", "slab"), P()),
        check_vma=False,
    )

    def program(tomogram, centers, owner, rotation, ctf, ref_spectra):
        box_len = ref_spectra.shape[2]
        plane = jnp.asarray(plane_tables(box_len))
        depth = jnp.asarray(depth_tables(box_len))
        return inner(tomogram, centers, owner, rotation, ctf, ref_spectra, plane, depth)

    return program
```

```python
import functools
import math

import jax
import jax.numpy as jnp
import ml_dtypes
import numpy as np
from jax import lax
from jax.experimental import pallas as pl
from jax.experimental.pallas import tpu as pltpu
from jax.sharding import PartitionSpec as P

GROUP = 8
LIMIT = 56 * 1024 * 1024


def split_table(table):
    high = table.astype(ml_dtypes.bfloat16)
    low = (table - high.astype(np.float64)).astype(ml_dtypes.bfloat16)
    return high, low


def plane_tables(length):
    n = np.arange(length)
    angles = 2.0 * math.pi / length * (np.outer(n, n) % length)
    one = (np.cos(angles) - 1j * np.sin(angles)) / math.sqrt(length)
    both = np.kron(one, one)
    table = np.concatenate((both.real, both.imag), axis=1)
    return np.stack(split_table(table))


def depth_tables(length):
    n = np.arange(length)
    angles = 2.0 * math.pi / length * (np.outer(n, n) % length)
    c = np.cos(angles) / math.sqrt(length)
    s = np.sin(angles) / math.sqrt(length)
    result = []
    for sign in (1.0, -1.0):
        high, low = split_table(np.block([[c, sign * s], [-sign * s, c]]))
        result.append(np.concatenate((high, high, low), axis=1))
    return np.stack(result)


def split(x):
    high = x.astype(jnp.bfloat16)
    return high, (x - high.astype(jnp.float32)).astype(jnp.bfloat16)


def dot(a, b):
    return jnp.dot(a, b, preferred_element_type=jnp.float32)


def depth_pass(table, x):
    high, low = split(x)
    return dot(table, jnp.concatenate((high, low, high), axis=0))


def cut_kernel(info, below, here, above, boxes, sums, volume, first, second):
    depth, rows, cols = here.shape
    slots, box_len, _ = boxes.shape
    span = box_len + 16
    half = below.shape[0]
    sums[...] = jnp.zeros_like(sums)
    volume[:half] = below[...]
    volume[half : half + depth] = here[...]
    volume[half + depth :] = above[...]
    lane = lax.broadcasted_iota(jnp.int32, (cols, 128), 1)
    source = lax.broadcasted_iota(jnp.int32, (cols, 128), 0)
    quarter = lax.broadcasted_iota(jnp.int32, (box_len, 128), 1) // box_len

    def cut(i, window):
        z0 = info[0, i]
        x0 = info[1, i]
        y0 = info[2, i]
        rot = info[3, i]
        live = info[4, i]
        start = pl.multiple_of(jnp.minimum(x0 // 16 * 16, rows - span), 16)
        pick = (source == y0 + lane % box_len).astype(jnp.float32).astype(jnp.bfloat16)
        cells = volume[pl.ds(z0, box_len), pl.ds(start, span), :]
        window[...] = dot(cells.reshape(box_len * span, cols), pick)
        shift = x0 - start
        for q in range(box_len * box_len // 128):
            part = jnp.zeros((box_len, 128), jnp.float32)
            for e in range(128 // box_len):
                got = window[pl.ds(shift + q * (128 // box_len) + e, box_len, stride=span), :]
                part = jnp.where(quarter == e, got, part)
            lanes = pl.ds(q * 128, 128)
            boxes[i, :, lanes] = part.astype(jnp.bfloat16)
            sums[rot, :box_len, lanes] += jnp.where(live > 0, part, 0.0)
        sums[rot, box_len:, :] += jnp.where(live > 0, 1.0, 0.0)

    @pl.loop(0, slots // 2)
    def _(pair):
        cut(2 * pair, first)
        cut(2 * pair + 1, second)


def score_kernel(rot, boxes, refs, ctf, plane, depth, out, spec, back_high, back_low):
    slots, box_len, cells = boxes.shape
    rows = GROUP * box_len

    @pl.loop(0, slots // GROUP)
    def _(g):
        b = boxes[pl.ds(g * GROUP, GROUP)].reshape(rows, cells)
        spec[...] = (dot(b, plane[0]) + dot(b, plane[1])).reshape(GROUP, box_len, 2 * cells)

        powers = []
        for j in range(GROUP):
            slot = g * GROUP + j
            ref_at = rot[slot]
            x = spec[j]
            x = jnp.concatenate((x[:, :cells], x[:, cells:]), axis=0)
            x = depth_pass(depth[0], x)
            weights = ctf[...]
            sr = x[:box_len] * weights
            si = x[box_len:] * weights
            rr = refs[ref_at, 0]
            ri = refs[ref_at, 1]
            own = jnp.sum(sr * sr + si * si, axis=(0, 1), keepdims=True)
            ref = jnp.sum(rr * rr + ri * ri, axis=(0, 1), keepdims=True)
            powers.append(own * ref)
            prod = jnp.concatenate((sr * rr + si * ri, si * rr - sr * ri), axis=0)
            high, low = split(depth_pass(depth[1], prod))
            at = pl.ds(j * box_len, box_len)
            back_high[at, :cells] = high[:box_len]
            back_high[at, cells:] = high[box_len:]
            back_low[at, :cells] = low[:box_len]
            back_low[at, cells:] = low[box_len:]

        cross = jnp.zeros((rows, cells), jnp.float32)
        for c in range(2):
            lanes = pl.ds(c * cells, cells)
            high = back_high[:, lanes]
            cross += dot(high, plane[0, :, lanes]) + dot(high, plane[1, :, lanes])
            cross += dot(back_low[:, lanes], plane[0, :, lanes])
        for j in range(GROUP):
            part = cross[j * box_len : (j + 1) * box_len]
            peak = jnp.max(part, axis=(0, 1), keepdims=True)
            score = (cells * box_len) * peak / jnp.sqrt(powers[j] + 1e-06)
            out[pl.ds(g * GROUP + j, 1), :] = jnp.broadcast_to(score, (1, 128))


def class_kernel(sums, ctf, plane, depth, out):
    count = sums.shape[0]
    box_len, cells = ctf.shape
    high, low = split(sums[:, :box_len, :].reshape(count * box_len, cells))
    x = dot(high, plane[0]) + dot(high, plane[1]) + dot(low, plane[0])
    for r in range(count):
        part = x[r * box_len : (r + 1) * box_len]
        part = jnp.concatenate((part[:, :cells], part[:, cells:]), axis=0)
        part = depth_pass(depth[0], part)
        at = pl.ds(r * box_len, box_len)
        out[0, at, :] = part[:box_len] * ctf[...]
        out[1, at, :] = part[box_len:] * ctf[...]
        out[2, at, :] = sums[r, box_len : box_len + 1, :] * ctf[...] * ctf[...]


def gather_kernel(slabs, tomos, chunk, labels, out, tags, send, arrive, tag_send, tag_arrive, local_sems):
    s = lax.axis_index("slab")
    t = lax.axis_index("tomo")
    pairs = slabs // 2
    parity = lax.rem(s, 2)
    pair = s // 2
    sibling = s + 1 - 2 * parity
    peers = [lax.rem(pair + d, pairs) * 2 + parity for d in range(1, pairs)]
    depths = [lax.rem(t + d, tomos) for d in range(1, tomos)]
    mates = [lax.rem(s + d, slabs) for d in range(1, slabs)]

    barrier = pltpu.get_barrier_semaphore()
    partners = [(s, d) for d in depths] + [(m, t) for m in mates]
    for place in partners:
        pl.semaphore_signal(barrier, inc=1, device_id=place, device_id_type=pl.DeviceIdType.MESH)
    pl.semaphore_wait(barrier, len(partners))

    started = []

    def push(source, at_s, at_t, place):
        copy = pltpu.make_async_remote_copy(
            src_ref=source,
            dst_ref=out.at[at_s, at_t],
            send_sem=send.at[len(started)],
            recv_sem=arrive.at[at_s, at_t],
            device_id=place,
            device_id_type=pl.DeviceIdType.MESH,
        )
        copy.start()
        started.append(copy)

    def landed(at_s, at_t):
        pltpu.make_async_remote_copy(
            src_ref=out.at[at_s, at_t],
            dst_ref=out.at[at_s, at_t],
            send_sem=send.at[0],
            recv_sem=arrive.at[at_s, at_t],
            device_id=(sibling, t),
            device_id_type=pl.DeviceIdType.MESH,
        ).wait_recv()

    own = pltpu.make_async_copy(chunk, out.at[s, t], local_sems.at[0])
    own.start()
    own_tag = pltpu.make_async_copy(labels, tags.at[s], local_sems.at[1])
    own_tag.start()
    for d in depths:
        push(chunk, s, t, (s, d))
    for p in peers:
        push(chunk, s, t, (p, t))
    push(chunk, s, t, (sibling, t))
    tag_copies = []
    for i, m in enumerate(mates):
        copy = pltpu.make_async_remote_copy(
            src_ref=labels,
            dst_ref=tags.at[s],
            send_sem=tag_send.at[i],
            recv_sem=tag_arrive.at[s],
            device_id=(m, t),
            device_id_type=pl.DeviceIdType.MESH,
        )
        copy.start()
        tag_copies.append(copy)
    for d in depths:
        landed(s, d)
        for p in peers:
            push(out.at[s, d], s, d, (p, t))
        push(out.at[s, d], s, d, (sibling, t))
    for d in [t] + depths:
        for p in peers:
            landed(p, d)
            push(out.at[p, d], p, d, (sibling, t))
    for d in [t] + depths:
        for p in [pair * 2 + 1 - parity] + [q + 1 - 2 * parity for q in peers]:
            landed(p, d)
    for m in mates:
        pltpu.make_async_remote_copy(
            src_ref=labels,
            dst_ref=tags.at[m],
            send_sem=tag_send.at[0],
            recv_sem=tag_arrive.at[m],
            device_id=(m, t),
            device_id_type=pl.DeviceIdType.MESH,
        ).wait_recv()
    own.wait()
    own_tag.wait()
    for copy in started + tag_copies:
        copy.wait_send()


VMEM = pl.BlockSpec(memory_space=pltpu.VMEM)
SMEM = pl.BlockSpec(memory_space=pltpu.SMEM)
ANY = pl.BlockSpec(memory_space=pl.ANY)


def local(tomogram, centers, owner, rotation, ctf, ref_spectra, plane, depth):
    slab_count = lax.axis_size("slab")
    tomo_count = lax.axis_size("tomo")
    me = lax.axis_index("slab")
    ref_count, _, box_len, cells = ref_spectra.shape
    half = box_len // 2
    here = tomogram[0]
    slab_depth, rows, cols = here.shape
    slots = owner.shape[1]
    aligned = 16

    n = slab_count
    below = lax.ppermute(here[slab_depth - half :], "slab", [(i, i + 1) for i in range(n - 1)])
    above = lax.ppermute(here[:half], "slab", [(i + 1, i) for i in range(n - 1)])

    info = jnp.stack(
        (
            centers[0, 0] - me * slab_depth,
            centers[0, 1] - half,
            centers[0, 2] - half,
            rotation[0],
            (owner[0] >= 0).astype(jnp.int32),
        )
    )
    boxes, sums = pl.pallas_call(
        cut_kernel,
        out_shape=(
            jax.ShapeDtypeStruct((slots, box_len, cells), jnp.bfloat16),
            jax.ShapeDtypeStruct((ref_count, box_len + 8, cells), jnp.float32),
        ),
        in_specs=[SMEM, VMEM, VMEM, VMEM],
        out_specs=(VMEM, VMEM),
        scratch_shapes=[
            pltpu.VMEM((2 * half + slab_depth, rows, cols), jnp.bfloat16),
            pltpu.VMEM((box_len * (box_len + 16), 128), jnp.float32),
            pltpu.VMEM((box_len * (box_len + 16), 128), jnp.float32),
        ],
        compiler_params=pltpu.CompilerParams(vmem_limit_bytes=LIMIT),
    )(info, below, here, above)

    mine = lax.psum_scatter(sums, "slab", scatter_dimension=0, tiled=True)

    score_call = lambda part: pl.pallas_call(
        score_kernel,
        out_shape=jax.ShapeDtypeStruct((part, 128), jnp.float32),
        in_specs=[SMEM, VMEM, VMEM, VMEM, VMEM, VMEM],
        out_specs=VMEM,
        scratch_shapes=[
            pltpu.VMEM((GROUP, box_len, 2 * cells), jnp.float32),
            pltpu.VMEM((GROUP * box_len, 2 * cells), jnp.bfloat16),
            pltpu.VMEM((GROUP * box_len, 2 * cells), jnp.bfloat16),
        ],
        compiler_params=pltpu.CompilerParams(vmem_limit_bytes=LIMIT),
        cost_estimate=pl.CostEstimate(
            flops=2 * part * box_len * cells * 2 * cells * 8, bytes_accessed=20 << 20, transcendentals=0
        ),
    )
    def score_part(i, length):
        return score_call(length)(
            rotation[0, i : i + length], boxes[i : i + length], ref_spectra, ctf[0], plane, depth
        )[:, 0]

    part = slots * 3 // 4
    early = score_part(0, part)
    mine, early = lax.optimization_barrier((mine, early))

    count = ref_count // slab_count
    spectra = pl.pallas_call(
        class_kernel,
        out_shape=jax.ShapeDtypeStruct((3, count * box_len, cells), jnp.float32),
        in_specs=[VMEM] * 4,
        out_specs=VMEM,
        compiler_params=pltpu.CompilerParams(vmem_limit_bytes=LIMIT),
        cost_estimate=pl.CostEstimate(
            flops=2 * count * box_len * cells * 2 * cells * 4, bytes_accessed=10 << 20, transcendentals=0
        ),
    )(mine, ctf[0], plane, depth)
    numer = lax.psum_scatter(spectra, "tomo", scatter_dimension=1, tiled=True)
    scores = jnp.concatenate((early, score_part(part, slots - part)))

    per = count * box_len // tomo_count
    result = numer[:2] / (numer[2:] + 1.0)

    largest = jnp.max(jnp.abs(result), axis=2, keepdims=True)
    power = jnp.floor(jnp.log2(jnp.maximum(largest, 2.0**-90))) - 13.0
    digits = jnp.ceil(largest / jnp.exp2(power))

    def row_scale(digits, power):
        return jnp.maximum(digits, 1.0) * jnp.exp2(power) * (1.0 / 32767.0)

    coded = jnp.clip(jnp.round(result / row_scale(digits, power)), -32767.0, 32767.0)
    lane = lax.broadcasted_iota(jnp.int32, (2, per, 128), 2)
    coded = jnp.concatenate((coded, jnp.where(lane == 0, digits, power)), axis=2)
    coded = coded.astype(jnp.int16).reshape(2 * per, cells + 128)
    labels = jnp.zeros((8, 128), jnp.float32).at[0, :slots].set(scores)
    labels = labels.at[1, :slots].set(owner[0].astype(jnp.float32))
    pairs = slab_count // 2
    sends = tomo_count - 1 + pairs + (tomo_count - 1) * pairs + tomo_count * (pairs - 1)
    gathered, tags = pl.pallas_call(
        functools.partial(gather_kernel, slab_count, tomo_count),
        out_shape=(
            jax.ShapeDtypeStruct((slab_count, tomo_count, 2 * per, cells + 128), jnp.int16),
            jax.ShapeDtypeStruct((slab_count, 8, 128), jnp.float32),
        ),
        in_specs=[ANY, ANY],
        out_specs=(ANY, ANY),
        scratch_shapes=[
            pltpu.SemaphoreType.DMA((sends,)),
            pltpu.SemaphoreType.DMA((slab_count, tomo_count)),
            pltpu.SemaphoreType.DMA((slab_count,)),
            pltpu.SemaphoreType.DMA((slab_count,)),
            pltpu.SemaphoreType.DMA((2,)),
        ],
        compiler_params=pltpu.CompilerParams(
            collective_id=0, has_side_effects=True, vmem_limit_bytes=LIMIT
        ),
    )(coded, labels)
    gathered = gathered.reshape(ref_count, box_len // per, 2, per, cells + 128)
    head = gathered[..., cells : cells + 2].astype(jnp.float32)
    scale = row_scale(head[..., :1], head[..., 1:])
    decoded = gathered[..., :cells].astype(jnp.float32) * scale
    new_reference = jnp.swapaxes(decoded, 1, 2).reshape(ref_count, 2, box_len, cells)

    all_scores = tags[:, 0, :slots].reshape(slab_count * slots)
    own = tags[:, 1, :slots].reshape(slab_count * slots).astype(jnp.int32) == me
    rank = jnp.cumsum(own.astype(jnp.int32)) - 1
    chosen = own[None, :] & (rank[None, :] == jnp.arange(aligned, dtype=jnp.int32)[:, None])
    score = jnp.sum(jnp.where(chosen, all_scores[None, :], 0.0), axis=1)
    return score.reshape(1, aligned), new_reference


def solution(mesh):
    inner = jax.shard_map(
        local,
        mesh=mesh,
        in_specs=(
            P("tomo", "slab", None, None),
            P("tomo", None, "slab"),
            P("tomo", "slab"),
            P("tomo", "slab"),
            P("tomo", None, None),
            P(),
            P(),
            P(),
        ),
        out_specs=(P("tomo", "slab"), P()),
        check_vma=False,
    )

    def program(tomogram, centers, owner, rotation, ctf, ref_spectra):
        box_len = ref_spectra.shape[2]
        plane = jnp.asarray(plane_tables(box_len))
        depth = jnp.asarray(depth_tables(box_len))
        return inner(tomogram, centers, owner, rotation, ctf, ref_spectra, plane, depth)

    return program
```
